512 devices in a mesh: gx: 16 (over y_lo, x, core), gy: 32 (over z, y_hi).
Axes of the slice: x: 4, y: 4 (y_hi: 2, y_lo: 2; y = y_hi * 2 + y_lo), z: 16, core: 2. Of those that a mesh axis runs over, the one named last changes fastest.
Arguments:
- forcing: float32 [64, 64, 2, 4096], P('gx', 'gy'), may hold values from -6 to 6
- initial: float32 [64, 64, 2, 4096], P('gx', 'gy'), may hold values from -6 to 6
- blocks: float32 [64, 64, 2, 4096], P('gx', 'gy'), as said below
- face_blocks: float32 [6, 64, 64], replicated, may hold values from -0.75 to 0.75
- strength: float32 [6, 64, 64, 2], P(None, 'gx', 'gy'), may hold values from 0.2 to 2
- strong: int32 [6, 64, 64, 2], P(None, 'gx', 'gy'), may hold values 0 or 1
- colour: int32 [64, 64, 2], P('gx', 'gy'), may hold values from 0 to 1, as said below
- neighbours: int32 [6, 64, 64, 2], P(None, 'gx', 'gy'), may hold values from 2 to 48, as said below
Outputs:
- smoothed: float32 [64, 64, 2, 4096], P('gx', 'gy')
The draws below stay inside these ranges and needn't reach their ends.
Inputs may be any that keep to these rules, and one draw needn't show every extreme that they name: Elements of a column along z are stored in an order drawn per column. colour is (global x index + global y index + physical position along z + one flip common to all elements) mod 2, so elements that share a face differ in colour and every column holds one element of each colour. `neighbours`: each entry is the slot, in the extended block of the device holding the element, of the element across that face, as in the reference program; faces on the domain's boundary hold 48. Slots of the four corner columns are never named. `blocks`: each block is symmetric, and each diagonal entry exceeds the sum of the magnitudes of the other entries of its row by 0.5 or more.
All inputs are finite; a program needn't handle non-finite values. No bound on the sum of `strong` on one device may be relied on, other than what follows from the above.
Results may differ from the reference program's by a relative error of at most 0.00011.
Values sent between devices are 32-bit elements; how exact they have to be, the bound alone decides.
A program may use at most 64 MiB of HBM per device.

```python
import math
import jax
import jax.numpy as jnp
from jax import lax

P_SIZE = 64
R = 64
EX = 4
EY = 2
EZ = 2
SWEEPS = 4
NX = 64
NY = 64


def column_layout(key):
    seeded = jax.random.fold_in(key, 7)
    scores = jax.random.randint(seeded, (NX, NY, EZ), 0, 1 << 20)
    distinct = scores * EZ + jnp.arange(EZ, dtype=jnp.int32)
    placed = jnp.argsort(distinct, axis=2, stable=True).astype(jnp.int32)
    slot_of = jnp.argsort(placed, axis=2, stable=True).astype(jnp.int32)
    parity_flip = jax.random.randint(jax.random.fold_in(seeded, 1), (), 0, 2)
    return (placed, slot_of, parity_flip)


def draw_colour(key, part):
    placed, slot_of, parity_flip = column_layout(key)
    grid_x = jnp.arange(NX, dtype=jnp.int32)[:, None, None]
    grid_y = jnp.arange(NY, dtype=jnp.int32)[None, :, None]
    return ((grid_x + grid_y + placed + parity_flip) % 2).astype(jnp.int32)


def draw_neighbours(key, part):
    placed, slot_of, parity_flip = column_layout(key)
    empty_slot = (EX + 2) * (EY + 2) * EZ
    grid_x = jnp.arange(NX, dtype=jnp.int32)[:, None, None]
    grid_y = jnp.arange(NY, dtype=jnp.int32)[None, :, None]
    local_x = grid_x % EX
    local_y = grid_y % EY

    def position(ext_a, ext_b, stored):
        return (ext_a * (EY + 2) + ext_b) * EZ + stored

    def lookup(slots, depth):
        return jnp.take_along_axis(slots, depth, axis=2)
    before_x = jnp.concatenate([slot_of[:1], slot_of[:-1]], axis=0)
    after_x = jnp.concatenate([slot_of[1:], slot_of[-1:]], axis=0)
    before_y = jnp.concatenate([slot_of[:, :1], slot_of[:, :-1]], axis=1)
    after_y = jnp.concatenate([slot_of[:, 1:], slot_of[:, -1:]], axis=1)
    lower_z = jnp.maximum(placed - 1, 0)
    upper_z = jnp.minimum(placed + 1, EZ - 1)
    by_face = [jnp.where(grid_x > 0, position(local_x, local_y + 1, lookup(before_x, placed)), empty_slot), jnp.where(grid_x < NX - 1, position(local_x + 2, local_y + 1, lookup(after_x, placed)), empty_slot), jnp.where(grid_y > 0, position(local_x + 1, local_y, lookup(before_y, placed)), empty_slot), jnp.where(grid_y < NY - 1, position(local_x + 1, local_y + 2, lookup(after_y, placed)), empty_slot), jnp.where(placed > 0, position(local_x + 1, local_y + 1, lookup(slot_of, lower_z)), empty_slot), jnp.where(placed < EZ - 1, position(local_x + 1, local_y + 1, lookup(slot_of, upper_z)), empty_slot)]
    return jnp.stack(by_face).astype(jnp.int32)


def draw_blocks(key, part):
    seeded = jax.random.fold_in(key, 3)
    first_key, second_key = jax.random.split(seeded)
    spread = jnp.exp(jax.random.uniform(first_key, (NX, NY, EZ, P_SIZE), jnp.float32, jnp.log(0.2), jnp.log(4.0)))
    random_part = jax.random.uniform(second_key, (NX, NY, EZ, P_SIZE, P_SIZE), jnp.float32, -1.0, 1.0) / P_SIZE
    symmetric = 0.5 * (random_part + jnp.swapaxes(random_part, -1, -2))
    rows_index = jnp.arange(P_SIZE, dtype=jnp.int32)[:, None]
    cols_index = jnp.arange(P_SIZE, dtype=jnp.int32)[None, :]
    on_diagonal = (rows_index == cols_index).astype(jnp.float32)
    matrices = symmetric * (1.0 - on_diagonal) + on_diagonal * (1.5 + spread)[..., None]
    return matrices.reshape(NX, NY, EZ, P_SIZE * P_SIZE)


def place_ends(drawn, stream_key, least, high):
    index_at = [jax.random.randint(jax.random.fold_in(stream_key, axis), (), 0, length) for axis, length in enumerate(drawn.shape)]
    widest = drawn.shape.index(max(drawn.shape))
    next_to = index_at[:widest] + [(index_at[widest] + 1) % drawn.shape[widest]] + index_at[widest + 1:]
    return drawn.at[tuple(index_at)].set(least).at[tuple(next_to)].set(high)


def levels(own_key, extent, cuts, least, top_value):
    loudness = 1.0
    for dim, shards_of in cuts:
        draws = jax.random.uniform(jax.random.fold_in(jax.random.fold_in(own_key, 6), dim), (shards_of,), jnp.float32, least / len(cuts), top_value / len(cuts))
        loudness = loudness * jnp.repeat(jnp.exp(draws), extent[dim] // shards_of).reshape((-1,) + (1,) * (len(extent) - 1 - dim))
    return loudness


def noise(key, extent, deviation, reach, cuts=(), held_as=jnp.bfloat16):
    entries = jax.random.normal(key, extent, jnp.float32) * deviation
    if len(cuts) > 0:
        entries = levels(key, extent, cuts, -0.22, 0.18) * entries
    return jnp.clip(entries, min=-reach, max=reach).astype(held_as)


def setup_inputs(seed: int = 0) -> dict:
    arg_keys = jax.random.split(jax.random.key(seed), 9)
    forcing = noise(arg_keys[0], (NX, NY, EZ, P_SIZE * R), 1.0, 6.0, ((0, 16), (1, 32)), jnp.float32)
    initial = noise(arg_keys[1], (NX, NY, EZ, P_SIZE * R), 1.0, 6.0, ((0, 16), (1, 32)), jnp.float32)
    blocks = draw_blocks(jax.random.fold_in(arg_keys[8], 71), 0)
    face_blocks = noise(arg_keys[3], (6, P_SIZE, P_SIZE), P_SIZE ** -0.5, 0.75, (), jnp.float32)
    strength = jnp.clip(jnp.exp(math.log(2.0) - 2.3025851 * jax.random.uniform(arg_keys[4], (6, NX, NY, EZ), jnp.float32) ** levels(arg_keys[4], (6, NX, NY, EZ), ((1, 16), (2, 32)), -0.2, 0.2)), 0.2, 2.0)
    strong = place_ends((jax.random.randint(arg_keys[5], (6, NX, NY, EZ), 0, 3) < 2).astype(jnp.int32), jax.random.fold_in(arg_keys[5], 1), 0, 1)
    colour = draw_colour(jax.random.fold_in(arg_keys[8], 71), 0)
    neighbours = draw_neighbours(jax.random.fold_in(arg_keys[8], 71), 0)
    return {"forcing": forcing, "initial": initial, "blocks": blocks, "face_blocks": face_blocks, "strength": strength, "strong": strong, "colour": colour, "neighbours": neighbours}


def global_rows(neighbours):
    whole_count = NX * NY * EZ
    empty_slot = (EX + 2) * (EY + 2) * EZ
    column_size = (EY + 2) * EZ
    ext_x = neighbours // column_size
    ext_y = neighbours // EZ % (EY + 2)
    ext_slot = neighbours % EZ
    grid_x = jnp.arange(NX, dtype=jnp.int32)[None, :, None, None]
    grid_y = jnp.arange(NY, dtype=jnp.int32)[None, None, :, None]
    target_x = grid_x // EX * EX + ext_x - 1
    target_y = grid_y // EY * EY + ext_y - 1
    flat_rows = (target_x * NY + target_y) * EZ + ext_slot
    return jnp.where(neighbours == empty_slot, whole_count, flat_rows).astype(jnp.int32)

def block_inverses(matrices):
    lower_factor = jnp.linalg.cholesky(matrices)
    identity = jnp.broadcast_to(jnp.eye(P_SIZE, dtype=matrices.dtype), matrices.shape)
    solved = jax.scipy.linalg.solve_triangular(lower_factor, identity, lower=True)
    return jnp.einsum('eqp,eqr->epr', solved, solved, precision=lax.Precision.HIGHEST)

def reference(forcing, initial, blocks, face_blocks, strength, strong, colour, neighbours):
    count = NX * NY * EZ
    inverse = block_inverses(blocks.reshape(count, P_SIZE, P_SIZE)).reshape(NX, NY * EZ, P_SIZE, P_SIZE)
    weight = (strength * strong.astype(strength.dtype)).reshape(6, NX, NY * EZ)
    weight_slabs = jnp.moveaxis(weight, 0, 1)
    row_slabs = jnp.moveaxis(global_rows(neighbours).reshape(6, NX, NY * EZ), 0, 1)
    target = forcing.reshape(NX, NY * EZ, P_SIZE, R)
    paint = colour.reshape(NX, NY * EZ)
    state = initial.reshape(count, P_SIZE, R)
    blank = jnp.zeros((1, P_SIZE, R), state.dtype)
    for sweep_index in range(SWEEPS):
        for paint_now in (0, 1):
            padded = jnp.concatenate([state, blank], axis=0)

            def one_slab(packed):
                rows_slab, weight_slab, target_slab, inverse_slab = packed
                coupled = jnp.zeros_like(target_slab)
                for face_index in range(6):
                    nearby = padded[rows_slab[face_index]]
                    product = jnp.einsum('pq,eqr->epr', face_blocks[face_index], nearby, precision=lax.Precision.HIGHEST)
                    coupled = coupled + weight_slab[face_index][:, None, None] * product
                return jnp.einsum('epq,eqr->epr', inverse_slab, target_slab - coupled, precision=lax.Precision.HIGHEST)
            update = lax.map(one_slab, (row_slabs, weight_slabs, target, inverse))
            current = state.reshape(NX, NY * EZ, P_SIZE, R)
            state = jnp.where((paint == paint_now)[..., None, None], update, current).reshape(count, P_SIZE, R)
    return state.reshape(NX, NY, EZ, P_SIZE * R)
```

```python
import jax
import jax.numpy as jnp
from jax import lax
from jax.experimental import pallas as pl
from jax.experimental.pallas import tpu as pltpu
from jax.sharding import PartitionSpec as P

MESH = pl.DeviceIdType.MESH
N = 64
STEPS = 8
F32 = jnp.float32
BF16 = jnp.bfloat16


def left_lanes(shape):
    return lax.broadcasted_iota(jnp.int32, shape, len(shape) - 1) < N


def swap(tile):
    return pltpu.roll(tile, N, tile.ndim - 1)


def parts(value):
    high = value.astype(BF16)
    return high, (value - high.astype(F32)).astype(BF16)


def unpack_pair(source, rows, store, bank, b, h, paint):
    halves = []
    for low in range(2):
        a = 2 * h + low
        first = rows[pl.ds(a * 2 + b, 1), pl.ds(6 * N, 128)] * jnp.ones((32, 1), F32)
        zero = source[a, b, pl.ds(0, 32, stride=2), :]
        one = source[a, b, pl.ds(1, 32, stride=2), :]
        wanted = first == paint
        halves.append(jnp.where(wanted, zero, one))
    left = left_lanes((32, 128))
    even = jnp.where(left, halves[0], swap(halves[1]))
    odd = jnp.where(left, swap(halves[0]), halves[1])
    store[bank, b, h, pl.ds(0, 32, stride=2), :] = even
    store[bank, b, h, pl.ds(1, 32, stride=2), :] = odd


def invert(grid):
    pairs = grid.shape[0]
    lane = lax.broadcasted_iota(jnp.int32, (8, 128), 1)
    row = lax.broadcasted_iota(jnp.int32, (8, 128), 0)
    within = lax.rem(lane, N)
    start = lane - within

    def pick(tile, index):
        return jnp.take_along_axis(tile, index, axis=1)

    def block(k, carry):
        panels = [grid[e, pl.ds(pl.multiple_of(8 * k, 8), 8), :] for e in range(pairs)]
        for j in range(8):
            column = 8 * k + j
            index = start + column
            here = within == column
            for e in range(pairs):
                panel = panels[e]
                pivot_row = jnp.broadcast_to(panel[j : j + 1, :], (8, 128))
                factor = pick(panel, index)
                scale = 1.0 / pick(pivot_row, index)
                scaled = jnp.where(here, 1.0, pivot_row) * scale
                rest = jnp.where(here, 0.0, panel) - factor * scaled
                panels[e] = jnp.where(row == j, scaled, rest)
        inside = (within >= 8 * k) & (within < 8 * k + 8)
        for e in range(pairs):
            panel = panels[e]

            def group(g, carry, e=e, panel=panel):
                at = pl.ds(pl.multiple_of(8 * g, 8), 8)
                old = grid[e, at, :]
                total = jnp.where(inside, 0.0, old)
                for j in range(8):
                    total = total - pick(old, start + 8 * k + j) * jnp.broadcast_to(
                        panel[j : j + 1, :], (8, 128)
                    )
                grid[e, at, :] = total
                return carry

            lax.fori_loop(0, 8, group, 0, unroll=True)
            grid[e, pl.ds(pl.multiple_of(8 * k, 8), 8), :] = panel
        return carry

    lax.fori_loop(0, 8, block, 0)


def kernel(
    forcing, initial, blocks, faces, rows, out,
    state, cross, halo, grid, couple, source_term, spread, send_sem, recv_sem,
):
    gx, gy = lax.axis_index("gx"), lax.axis_index("gy")
    nx, ny = lax.axis_size("gx"), lax.axis_size("gy")
    x_low, x_high = (lax.rem(gx + nx - 1, nx), gy), (lax.rem(gx + 1, nx), gy)
    y_low, y_high = (gx, lax.rem(gy + ny - 1, ny)), (gx, lax.rem(gy + 1, ny))
    barrier = pltpu.get_barrier_semaphore()
    for device in (x_low, x_high, y_low, y_high):
        pl.semaphore_signal(barrier, inc=1, device_id=device, device_id_type=MESH)
    left = left_lanes((N, 128))

    def copies(t):
        def copy(slot, source, device):
            return pltpu.make_async_remote_copy(
                src_ref=source,
                dst_ref=halo.at[t, slot],
                send_sem=send_sem.at[t, slot],
                recv_sem=recv_sem.at[t, slot],
                device_id=device,
                device_id_type=MESH,
            )

        return [
            copy(0, state.at[t, 1, 0], y_high),
            copy(1, state.at[t, 1, 1], y_high),
            copy(2, state.at[t, 0, 0], y_low),
            copy(3, state.at[t, 0, 1], y_low),
            copy(4, cross.at[t, 0], x_high),
            copy(5, cross.at[t, 1], x_low),
        ]

    def prepare(t):
        cross[t, 0] = jnp.where(left, swap(state[t, 0, 1]), state[t, 1, 1])
        cross[t, 1] = jnp.where(left, state[t, 0, 0], swap(state[t, 1, 0]))

    for b in range(2):
        for h in range(2):
            unpack_pair(initial, rows, state, 0, b, h, 0.0)
    prepare(0)
    pl.semaphore_wait(barrier, 4)
    for copy in copies(0):
        copy.start()

    for c in range(2):
        for b in range(2):
            for h in range(2):
                unpack_pair(blocks, rows, grid, c, b, h, 1.0 - c)
                unpack_pair(forcing, rows, source_term, c, b, h, 1.0 - c)
    invert(grid.reshape(8, N, 128))

    for i in range(3):
        both = jnp.concatenate([faces[2 * i], faces[2 * i + 1]], axis=1)
        high, low = parts(both)
        for half in range(2):
            at = pl.ds(half * N, N)
            spread[at, pl.ds(128 * i, 128)] = high
            spread[at, pl.ds(384 + 128 * i, 128)] = low

    def setup(i, carry):
        c, b, h = i // 4, lax.rem(i // 2, 2), lax.rem(i, 2)
        inverse = grid[c, b, h]
        stacked = jnp.concatenate(
            [jnp.where(left, inverse, 0.0), jnp.where(left, 0.0, inverse)], axis=0
        )
        high, low = parts(stacked)
        operand = jnp.concatenate([high, low], axis=0)
        folded = jnp.dot(operand, spread[...], preferred_element_type=F32)
        product = folded[:128, :384] + (folded[128:, :384] + folded[:128, 384:])
        target = source_term[c, b, h]
        t_high, t_low = parts(jnp.concatenate([target, target], axis=0))
        folded = jnp.dot(
            operand, jnp.concatenate([t_high, t_low], axis=1), preferred_element_type=F32
        )
        known = folded[:128, :128] + (folded[128:, :128] + folded[:128, 128:])
        source_term[c, b, h] = jnp.where(left, known[:N], known[N:])
        for low_x in range(2):
            e = c * 8 + (2 * h + low_x) * 2 + b
            scaled = product[N * low_x : N * low_x + N] * rows[pl.ds(e, 1), pl.ds(0, 384)]
            high, low = parts(scaled)
            couple[c, b, h, pl.ds(128 * low_x, N), :] = high
            couple[c, b, h, pl.ds(128 * low_x + N, N), :] = low
        return carry

    lax.fori_loop(0, 8, setup, 0)

    def step(t, c):
        for copy in copies(t):
            copy.wait_recv()
        x_before, x_after = halo[t, 4], halo[t, 5]
        for b in range(2):
            one, two = state[t, b, 0], state[t, b, 1]
            if b == 0:
                before, after = x_before, swap(x_after)
            else:
                before, after = swap(x_before), x_after
            slides = [
                jnp.where(left, before, swap(one)),
                swap(jnp.where(left, two, one)),
                jnp.where(left, swap(two), after),
            ]
            for h in range(2):
                y_before = halo[t, h] if b == 0 else state[t, 0, h]
                y_after = state[t, 1, h] if b == 0 else halo[t, 2 + h]
                own = state[t, b, h]
                near = jnp.concatenate(
                    [slides[h], slides[h + 1], y_before, y_after, own, own], axis=0
                )
                high, low = parts(near)
                total = jnp.dot(
                    couple[c, b, h],
                    jnp.concatenate([high, low], axis=1),
                    preferred_element_type=F32,
                )
                first = total[:N, :128] + (total[N:128, :128] + total[:N, 128:])
                second = total[128:192, :128] + (total[192:, :128] + total[128:192, 128:])
                state[t + 1, b, h] = source_term[c, b, h] - jnp.where(left, first, second)

    def sweep(t, carry):
        step(t, lax.rem(t, 2))
        prepare(t + 1)
        for copy in copies(t + 1):
            copy.start()
        return carry

    lax.fori_loop(0, STEPS - 1, sweep, 0)
    step(STEPS - 1, 1)

    small = left_lanes((32, 128))
    for b in range(2):
        for h in range(2):
            values = []
            for c in range(2):
                even = state[STEPS - 1 + c, b, h, pl.ds(0, 32, stride=2), :]
                odd = state[STEPS - 1 + c, b, h, pl.ds(1, 32, stride=2), :]
                values.append(
                    (jnp.where(small, even, swap(odd)), jnp.where(small, swap(even), odd))
                )
            for low_x in range(2):
                a = 2 * h + low_x
                first = rows[pl.ds(a * 2 + b, 1), pl.ds(6 * N, 128)] * jnp.ones((32, 1), F32)
                zero, one = values[0][low_x], values[1][low_x]
                out[a, b, pl.ds(0, 32, stride=2), :] = jnp.where(first == 1.0, zero, one)
                out[a, b, pl.ds(1, 32, stride=2), :] = jnp.where(first == 1.0, one, zero)

    def drain(t, carry):
        for copy in copies(t):
            copy.wait_send()
        return carry

    lax.fori_loop(0, STEPS, drain, 0)


def body(forcing, initial, blocks, face_blocks, strength, strong, colour, neighbours):
    sx, sy, sz, width = forcing.shape
    chunks = width // 128

    def packed(array):
        split = array.reshape(sx, sy, sz, chunks, 128).transpose(0, 1, 3, 2, 4)
        return split.reshape(sx, sy, chunks * sz, 128)

    weight = jnp.where(neighbours == 48, 0.0, strength * strong.astype(F32))
    zero_first = (colour[:, :, 0] == 0)[None]
    by_colour = jnp.stack(
        [
            jnp.where(zero_first, weight[..., 0], weight[..., 1]),
            jnp.where(zero_first, weight[..., 1], weight[..., 0]),
        ]
    )
    rows = jnp.repeat(by_colour.transpose(0, 2, 3, 1).reshape(16, 6), N, axis=1)
    first = jnp.broadcast_to(zero_first[0].astype(F32).reshape(1, 8, 1), (2, 8, 128))
    rows = jnp.concatenate([rows, first.reshape(16, 128)], axis=1)

    vmem = pl.BlockSpec(memory_space=pltpu.VMEM)
    result = pl.pallas_call(
        kernel,
        out_shape=jax.ShapeDtypeStruct((sx, sy, chunks * sz, 128), F32),
        in_specs=[vmem] * 5,
        out_specs=vmem,
        scratch_shapes=[
            pltpu.VMEM((STEPS + 1, 2, 2, N, 128), F32),
            pltpu.VMEM((STEPS, 2, N, 128), F32),
            pltpu.VMEM((STEPS, 6, N, 128), F32),
            pltpu.VMEM((2, 2, 2, N, 128), F32),
            pltpu.VMEM((2, 2, 2, 4 * N, 6 * N), BF16),
            pltpu.VMEM((2, 2, 2, N, 128), F32),
            pltpu.VMEM((2 * N, 12 * N), BF16),
            pltpu.SemaphoreType.DMA((STEPS, 6)),
            pltpu.SemaphoreType.DMA((STEPS, 6)),
        ],
        compiler_params=pltpu.CompilerParams(
            collective_id=0, has_side_effects=True, vmem_limit_bytes=40 * 2**20
        ),
    )(packed(forcing), packed(initial), packed(blocks), face_blocks, rows)
    result = result.reshape(sx, sy, chunks, sz, 128).transpose(0, 1, 3, 2, 4)
    return result.reshape(sx, sy, sz, width)


def solution(mesh):
    in_specs = (
        P("gx", "gy", None, None),
        P("gx", "gy", None, None),
        P("gx", "gy", None, None),
        P(),
        P(None, "gx", "gy", None),
        P(None, "gx", "gy", None),
        P("gx", "gy", None),
        P(None, "gx", "gy", None),
    )
    out_specs = P("gx", "gy", None, None)
    return jax.shard_map(body, mesh=mesh, in_specs=in_specs, out_specs=out_specs, check_vma=False)
```

```python
import jax
import jax.numpy as jnp
from jax import lax
from jax.experimental import pallas as pl
from jax.experimental.pallas import tpu as pltpu
from jax.sharding import PartitionSpec as P

MESH = pl.DeviceIdType.MESH
N = 64
STEPS = 8
GREET = 2
F32 = jnp.float32
BF16 = jnp.bfloat16


def left_lanes(shape):
    return lax.broadcasted_iota(jnp.int32, shape, len(shape) - 1) < N


def swap(tile):
    return pltpu.roll(tile, N, tile.ndim - 1)


def pick(tile, index):
    return jnp.take_along_axis(tile, index, axis=1)


def spread_row(tile, j):
    return jnp.broadcast_to(tile[j : j + 1, :], tile.shape)


def parts(value):
    high = value.astype(BF16)
    return high, (value - high.astype(F32)).astype(BF16)


def product(operand, value):
    high, low = parts(value)
    total = jnp.dot(
        operand, jnp.concatenate([high, low], axis=1), preferred_element_type=F32
    )
    first = total[:N, :128] + (total[N:128, :128] + total[:N, 128:])
    second = total[128:192, :128] + (total[192:, :128] + total[128:192, 128:])
    return jnp.where(left_lanes((N, 128)), first, second)


def unpack_pair(source, rows, target, b, h, paint):
    halves = []
    for low in range(2):
        a = 2 * h + low
        first = jnp.broadcast_to(rows[pl.ds(a * 2 + b, 1), pl.ds(384, 128)], (32, 128))
        zero = source[a, b, pl.ds(0, 32, stride=2), :]
        one = source[a, b, pl.ds(1, 32, stride=2), :]
        halves.append(jnp.where(first == paint, zero, one))
    left = left_lanes((32, 128))
    target[b, h, pl.ds(0, 32, stride=2), :] = jnp.where(left, halves[0], swap(halves[1]))
    target[b, h, pl.ds(1, 32, stride=2), :] = jnp.where(left, swap(halves[0]), halves[1])


def invert(grid, visit):
    places = [(b, h) for b in range(2) for h in range(2)]
    lane = lax.broadcasted_iota(jnp.int32, (8, 128), 1)
    row = lax.broadcasted_iota(jnp.int32, (8, 128), 0)
    within = lax.rem(lane, N)
    start = lane - within
    segment = within // 16

    def block(k, carry):
        visit(k)
        here = pl.ds(pl.multiple_of(8 * k, 8), 8)
        panels = [grid[b, h, here, :] for b, h in places]
        columns = []
        for j in range(8):
            index = start + 8 * k + j
            column = pick(panels[3], index)
            for e in range(3):
                column = jnp.where(segment == e, pick(panels[e], index), column)
            columns.append(column)
        for k2 in range(8):
            pivots = [spread_row(column, k2) for column in columns]
            scale = 1.0 / pivots[k2]
            factor = columns[k2]
            for j in range(8):
                scaled = scale if j == k2 else pivots[j] * scale
                rest = -(factor * scaled) if j == k2 else columns[j] - factor * scaled
                columns[j] = jnp.where(row == k2, scaled, rest)
        inside = (within >= 8 * k) & (within < 8 * k + 8)
        ones = within - 8 * k
        for e, (b, h) in enumerate(places):
            own = [pick(column, start + 16 * e) for column in columns]
            panel = jnp.zeros((8, 128), F32)
            for j in range(8):
                value = jnp.where(inside, 0.0, spread_row(panels[e], j))
                value = jnp.where(ones == j, 1.0, value)
                panel = panel + own[j] * value
            lines = [spread_row(panel, j) for j in range(8)]
            for g in range(8):
                at = pl.ds(8 * g, 8)
                old = grid[b, h, at, :]
                total = jnp.where(inside, 0.0, old)
                for j in range(8):
                    total = total - pick(old, start + 8 * k + j) * lines[j]
                grid[b, h, at, :] = total
            grid[b, h, here, :] = panel
        return carry

    lax.fori_loop(0, 8, block, 0)


def kernel(
    forcing_hbm, initial_hbm, blocks_hbm, faces_hbm, strength_hbm, strong_hbm, colour_hbm, near_hbm,
    out,
    forcing, initial, blocks, faces, strength, strong, colour, near, load_sem,
    rows, loose, state, cross, halo, grid, couple, known, partial, spread, send_sem, recv_sem,
):
    gx, gy = lax.axis_index("gx"), lax.axis_index("gy")
    nx, ny = lax.axis_size("gx"), lax.axis_size("gy")

    def device(dx, dy):
        return (lax.rem(gx + nx + dx, nx), lax.rem(gy + ny + dy, ny))

    def exists(dx, dy):
        return (gx + dx >= 0) & (gx + dx < nx) & (gy + dy >= 0) & (gy + dy < ny)

    sides = ((-1, 0), (1, 0), (0, -1), (0, 1))
    barrier = pltpu.get_barrier_semaphore()
    for side in sides:

        @pl.when(exists(*side))
        def _(side=side):
            pl.semaphore_signal(
                barrier, inc=1, device_id=device(*side), device_id_type=MESH
            )

    loads = [
        pltpu.make_async_copy(source, target, load_sem.at[i])
        for i, (source, target) in enumerate(
            [
                (strength_hbm, strength), (strong_hbm, strong), (colour_hbm, colour), (near_hbm, near),
                (initial_hbm, initial), (blocks_hbm, blocks), (forcing_hbm, forcing), (faces_hbm, faces),
            ]
        )
    ]
    for load in loads:
        load.start()

    left = left_lanes((N, 128))
    blank = jnp.zeros((N, 128), F32)

    def y_copy(t, b, h):
        slot = 2 * (1 - b) + h
        return pltpu.make_async_remote_copy(
            src_ref=state.at[t, b, h],
            dst_ref=halo.at[t, slot],
            send_sem=send_sem.at[t, slot],
            recv_sem=recv_sem.at[t, slot],
            device_id=device(0, 2 * b - 1),
            device_id_type=MESH,
        )

    def x_copy(t, side):
        return pltpu.make_async_remote_copy(
            src_ref=cross.at[t, side],
            dst_ref=halo.at[t, 5 - side],
            send_sem=send_sem.at[t, 5 - side],
            recv_sem=recv_sem.at[t, 5 - side],
            device_id=device(2 * side - 1, 0),
            device_id_type=MESH,
        )

    def y_start(t, b, h):
        @pl.when(exists(0, 2 * b - 1))
        def _():
            y_copy(t, b, h).start()

    def x_start(t):
        cross[t, 0] = jnp.where(left, state[t, 0, 0], swap(state[t, 1, 0]))
        cross[t, 1] = jnp.where(left, swap(state[t, 0, 1]), state[t, 1, 1])
        for side in range(2):

            @pl.when(exists(2 * side - 1, 0))
            def _(side=side):
                x_copy(t, side).start()

    nothing = jnp.zeros((STEPS, 2, N, 128), F32)
    for b in range(2):

        @pl.when(jnp.logical_not(exists(0, 2 * b - 1)))
        def _(b=b):
            halo[:, pl.ds(2 * b, 2)] = nothing

        @pl.when(jnp.logical_not(exists(2 * b - 1, 0)))
        def _(b=b):
            halo[:, 4 + b] = nothing[:, 0]

    for load in loads[:4]:
        load.wait()
    lane = lax.broadcasted_iota(jnp.int32, (8, 128), 1)
    column = lax.broadcasted_iota(jnp.int32, (8, 128), 0)
    loose[...] = jnp.zeros_like(loose)
    for a in range(4):
        for b in range(2):
            weight = jnp.where(
                near[a, b] == 48, 0.0, strength[a, b] * strong[a, b].astype(F32)
            )
            for s in range(2):
                loose[s, pl.ds(2 * a + b, 1), pl.ds(0, 6)] = weight[s : s + 1]
            loose[2, pl.ds(2 * a + b, 1), pl.ds(0, 4)] = colour[b, 0:1].astype(F32)
    painted = pick(loose[2], column // 2)
    for c in range(2):
        weight = jnp.where(painted == c, loose[0], loose[1])
        for i, face in enumerate((0, 4, 2)):
            rows[pl.ds(8 * c, 8), pl.ds(128 * i, 128)] = pick(weight, lane // N + face)
    rows[pl.ds(0, 8), pl.ds(384, 128)] = painted

    loads[4].wait()
    for b in range(2):
        for h in range(2):
            unpack_pair(initial, rows, state.at[0], b, h, 1.0)
    for load in loads[5:]:
        load.wait()
    for i, face in enumerate((0, 4, 2)):
        high, low = parts(jnp.concatenate([faces[face], faces[face + 1]], axis=1))
        for half in range(2):
            at = pl.ds(half * N, N)
            spread[at, pl.ds(128 * i, 128)] = high
            spread[at, pl.ds(384 + 128 * i, 128)] = low

    def greet():
        pl.semaphore_wait(barrier, sum(jnp.where(exists(*side), 1, 0) for side in sides))
        for b in range(2):
            for h in range(2):
                y_start(0, b, h)
        x_start(0)

    def setup(c):
        paint = c.astype(F32)
        for b in range(2):
            for h in range(2):
                unpack_pair(blocks, rows, grid, b, h, paint)
                unpack_pair(forcing, rows, known.at[c], b, h, paint)

        def visit(k):
            @pl.when((c == 0) & (k == GREET))
            def _():
                greet()

        invert(grid, visit)
        for b in range(2):
            for h in range(2):
                inverse = grid[b, h]
                stacked = jnp.concatenate(
                    [jnp.where(left, inverse, 0.0), jnp.where(left, 0.0, inverse)], axis=0
                )
                high, low = parts(stacked)
                operand = jnp.concatenate([high, low], axis=0)
                folded = jnp.dot(operand, spread[...], preferred_element_type=F32)
                mixed = folded[:128, :384] + (folded[128:, :384] + folded[:128, 384:])
                high, low = parts(known[c, b, h])
                target = jnp.concatenate([high, low], axis=1)
                folded = jnp.dot(
                    operand,
                    jnp.concatenate([target, target], axis=0),
                    preferred_element_type=F32,
                )
                mixed_known = folded[:128, :128] + (folded[128:, :128] + folded[:128, 128:])
                known[c, b, h] = jnp.where(left, mixed_known[:N], mixed_known[N:])
                for low_x in range(2):
                    weight = rows[pl.ds(8 * c + (2 * h + low_x) * 2 + b, 1), pl.ds(0, 384)]
                    scaled = mixed[N * low_x : N * low_x + N] * weight
                    if b == 0:
                        scaled = jnp.concatenate(
                            [scaled[:, :256], swap(scaled[:, 256:])], axis=1
                        )
                    high, low = parts(scaled)
                    couple[c, b, h, pl.ds(128 * low_x, N), :] = high
                    couple[c, b, h, pl.ds(128 * low_x + N, N), :] = low

    later = lax.rem(gy + 1, 2)

    def sweep(t, carry):
        c = lax.rem(t, 2)

        @pl.when(t < 2)
        def _():
            setup(c)

        for b in range(2):
            for h in range(2):
                own = state[t, b, h]
                beside = jnp.concatenate([own, own, state[t, 1 - b, h], blank], axis=0)
                partial[b, h] = known[c, b, h] - product(
                    couple[c, b, h, :, pl.ds(128, 256)], beside
                )
        for side in range(2):

            @pl.when(exists(2 * side - 1, 0))
            def _(side=side):
                x_copy(t, 1 - side).wait_recv()

        for b in range(2):
            one, two = state[t, b, 0], state[t, b, 1]
            before, after = halo[t, 4], halo[t, 5]
            if b == 0:
                after = swap(after)
            else:
                before = swap(before)
            slides = [
                jnp.where(left, before, swap(one)),
                swap(jnp.where(left, two, one)),
                jnp.where(left, swap(two), after),
            ]
            for h in range(2):
                beside = jnp.concatenate([slides[h], slides[h + 1]], axis=0)
                partial[b, h] = partial[b, h] - product(
                    couple[c, b, h, :, pl.ds(0, 128)], beside
                )
        for i in range(2):
            b = lax.rem(later + i, 2)

            @pl.when(exists(0, 2 * b - 1))
            def _(b=b):
                for h in range(2):
                    y_copy(t, 1 - b, h).wait_recv()

            for h in range(2):
                beside = jnp.concatenate([blank, halo[t, 2 * b + h]], axis=0)
                state[t + 1, b, h] = partial[b, h] - product(
                    couple[c, b, h, :, pl.ds(256, 128)], beside
                )

                @pl.when(t < STEPS - 1)
                def _(b=b, h=h):
                    y_start(t + 1, b, h)

        @pl.when(t < STEPS - 1)
        def _():
            x_start(t + 1)

        return carry

    lax.fori_loop(0, STEPS, sweep, 0)

    small = left_lanes((32, 128))
    for b in range(2):
        for h in range(2):
            values = []
            for c in range(2):
                even = state[STEPS - 1 + c, b, h, pl.ds(0, 32, stride=2), :]
                odd = state[STEPS - 1 + c, b, h, pl.ds(1, 32, stride=2), :]
                values.append(
                    (jnp.where(small, even, swap(odd)), jnp.where(small, swap(even), odd))
                )
            for low_x in range(2):
                a = 2 * h + low_x
                first = rows[pl.ds(a * 2 + b, 1), pl.ds(384, 128)]
                first = jnp.broadcast_to(first, (32, 128)) == 0.0
                zero, one = values[0][low_x], values[1][low_x]
                out[a, b, pl.ds(0, 32, stride=2), :] = jnp.where(first, zero, one)
                out[a, b, pl.ds(1, 32, stride=2), :] = jnp.where(first, one, zero)

    def drain(t, carry):
        for b in range(2):

            @pl.when(exists(0, 2 * b - 1))
            def _(b=b):
                for h in range(2):
                    y_copy(t, b, h).wait_send()

            @pl.when(exists(2 * b - 1, 0))
            def _(b=b):
                x_copy(t, b).wait_send()

        return carry

    lax.fori_loop(0, STEPS, drain, 0)


def body(forcing, initial, blocks, face_blocks, strength, strong, colour, neighbours):
    sx, sy, sz, width = forcing.shape
    chunks = width // 128

    def packed(array):
        split = array.reshape(sx, sy, sz, chunks, 128).transpose(0, 1, 3, 2, 4)
        return split.reshape(sx, sy, chunks * sz, 128)

    far = pl.BlockSpec(memory_space=pltpu.HBM)
    large = (sx, sy, chunks * sz, 128)
    result = pl.pallas_call(
        kernel,
        out_shape=jax.ShapeDtypeStruct(large, F32),
        in_specs=[far] * 8,
        out_specs=pl.BlockSpec(memory_space=pltpu.VMEM),
        scratch_shapes=[
            pltpu.VMEM(large, F32),
            pltpu.VMEM(large, F32),
            pltpu.VMEM(large, F32),
            pltpu.VMEM((6, N, N), F32),
            pltpu.VMEM((sx, sy, sz, 6), F32),
            pltpu.VMEM((sx, sy, sz, 6), jnp.int32),
            pltpu.VMEM((sy, sz, sx), jnp.int32),
            pltpu.VMEM((sx, sy, sz, 6), jnp.int32),
            pltpu.SemaphoreType.DMA((8,)),
            pltpu.VMEM((16, 512), F32),
            pltpu.VMEM((3, 8, 128), F32),
            pltpu.VMEM((STEPS + 1, 2, 2, N, 128), F32),
            pltpu.VMEM((STEPS, 2, N, 128), F32),
            pltpu.VMEM((STEPS, 6, N, 128), F32),
            pltpu.VMEM((2, 2, N, 128), F32),
            pltpu.VMEM((2, 2, 2, 4 * N, 6 * N), BF16),
            pltpu.VMEM((2, 2, 2, N, 128), F32),
            pltpu.VMEM((2, 2, N, 128), F32),
            pltpu.VMEM((2 * N, 12 * N), BF16),
            pltpu.SemaphoreType.DMA((STEPS, 6)),
            pltpu.SemaphoreType.DMA((STEPS, 6)),
        ],
        compiler_params=pltpu.CompilerParams(
            collective_id=0, has_side_effects=True, vmem_limit_bytes=65280 * 2**10
        ),
    )(
        packed(forcing),
        packed(initial),
        packed(blocks),
        face_blocks,
        strength.transpose(1, 2, 3, 0),
        strong.transpose(1, 2, 3, 0),
        colour.transpose(1, 2, 0),
        neighbours.transpose(1, 2, 3, 0),
    )
    result = result.reshape(sx, sy, chunks, sz, 128).transpose(0, 1, 3, 2, 4)
    return result.reshape(sx, sy, sz, width)


def solution(mesh):
    in_specs = (
        P("gx", "gy", None, None),
        P("gx", "gy", None, None),
        P("gx", "gy", None, None),
        P(),
        P(None, "gx", "gy", None),
        P(None, "gx", "gy", None),
        P("gx", "gy", None),
        P(None, "gx", "gy", None),
    )
    out_specs = P("gx", "gy", None, None)
    return jax.shard_map(body, mesh=mesh, in_specs=in_specs, out_specs=out_specs, check_vma=False)
```

```python
import jax
import jax.numpy as jnp
from jax import lax
from jax.experimental import pallas as pl
from jax.experimental.pallas import tpu as pltpu
from jax.sharding import PartitionSpec as P

MESH = pl.DeviceIdType.MESH
N = 64
STEPS = 8
GREET = 2
F32 = jnp.float32
BF16 = jnp.bfloat16


def left_lanes(shape):
    return lax.broadcasted_iota(jnp.int32, shape, len(shape) - 1) < N


def swap(tile):
    return pltpu.roll(tile, N, tile.ndim - 1)


def pick(tile, index):
    return jnp.take_along_axis(tile, index, axis=1)


def spread_row(tile, j):
    return jnp.broadcast_to(tile[j : j + 1, :], tile.shape)


def parts(value):
    high = value.astype(BF16)
    return high, (value - high.astype(F32)).astype(BF16)


def triple(value):
    high, low = parts(value)
    return jnp.concatenate([high, high, low], axis=0)


def product(operand, lines):
    total = jnp.dot(operand, lines, preferred_element_type=F32)
    return jnp.where(left_lanes((N, 128)), total[:N], total[N:])


def unpack_pair(source, rows, target, b, h, paint):
    halves = []
    for low in range(2):
        a = 2 * h + low
        first = jnp.broadcast_to(rows[pl.ds(a * 2 + b, 1), pl.ds(384, 128)], (32, 128))
        zero = source[a, b, pl.ds(0, 32, stride=2), :]
        one = source[a, b, pl.ds(1, 32, stride=2), :]
        halves.append(jnp.where(first == paint, zero, one))
    left = left_lanes((32, 128))
    target[b, h, pl.ds(0, 32, stride=2), :] = jnp.where(left, halves[0], swap(halves[1]))
    target[b, h, pl.ds(1, 32, stride=2), :] = jnp.where(left, swap(halves[0]), halves[1])


def invert(grid, visit):
    places = [(b, h) for b in range(2) for h in range(2)]
    lane = lax.broadcasted_iota(jnp.int32, (8, 128), 1)
    row = lax.broadcasted_iota(jnp.int32, (8, 128), 0)
    within = lax.rem(lane, N)
    start = lane - within
    segment = within // 16
    left = lane < N
    wide = lax.broadcasted_iota(jnp.int32, (N, 128), 1)
    slot = wide // 16
    first = (slot == 0) | (slot == 1) | (slot == 3)
    second = (slot == 2) | (slot == 4)
    third = slot == 5
    base = jnp.where(lax.rem(wide, 16) < 8, 0, N) + lax.rem(wide, 8)

    def block(k, carry):
        visit(k)
        here = pl.ds(pl.multiple_of(8 * k, 8), 8)
        panels = [grid[b, h, here, :] for b, h in places]
        columns = []
        for j in range(8):
            index = start + 8 * k + j
            column = pick(panels[3], index)
            for e in range(3):
                column = jnp.where(segment == e, pick(panels[e], index), column)
            columns.append(column)
        operands = []
        for b, h in places:
            value = pick(grid[b, h], base + 8 * k)
            part1 = value.astype(BF16).astype(F32)
            part2 = (value - part1).astype(BF16).astype(F32)
            part3 = value - part1 - part2
            operand = jnp.where(third, part3, 0.0)
            operand = jnp.where(first, part1, jnp.where(second, part2, operand))
            operands.append(operand.astype(BF16))
        for pivot in range(8):
            lines = [spread_row(column, pivot) for column in columns]
            scale = 1.0 / lines[pivot]
            factor = columns[pivot]
            for j in range(8):
                scaled = scale if j == pivot else lines[j] * scale
                rest = -(factor * scaled) if j == pivot else columns[j] - factor * scaled
                columns[j] = jnp.where(row == pivot, scaled, rest)
        inside = (within >= 8 * k) & (within < 8 * k + 8)
        inside_wide = (lax.rem(wide, N) >= 8 * k) & (lax.rem(wide, N) < 8 * k + 8)
        for e, (b, h) in enumerate(places):
            panel = jnp.zeros((8, 128), F32)
            for j in range(8):
                unit = jnp.where(within == 8 * k + j, 1.0, 0.0)
                value = jnp.where(inside, unit, spread_row(panels[e], j))
                panel = panel + pick(columns[j], start + 16 * e) * value
            both = jnp.concatenate(
                [jnp.where(left, panel, 0.0), jnp.where(left, 0.0, panel)], axis=0
            )
            part1 = both.astype(BF16)
            rest = both - part1.astype(F32)
            part2, part3 = parts(rest)
            nothing = jnp.zeros((32, 128), BF16)
            lines = jnp.concatenate(
                [part1, part2, part1, part3, part2, part1, nothing], axis=0
            )
            update = jnp.dot(operands[e], lines, preferred_element_type=F32)
            grid[b, h] = jnp.where(inside_wide, 0.0, grid[b, h]) - update
            grid[b, h, here, :] = panel
        return carry

    lax.fori_loop(0, 8, block, 0)


def kernel(
    forcing_hbm, initial_hbm, blocks_hbm, faces_hbm, strength_hbm, strong_hbm, colour_hbm, near_hbm,
    out,
    forcing, initial, blocks, faces, strength, strong, colour, near, load_sem,
    rows, loose, state, cross, halo, grid, couple, known, partial, spread, send_sem, recv_sem,
):
    gx, gy = lax.axis_index("gx"), lax.axis_index("gy")
    nx, ny = lax.axis_size("gx"), lax.axis_size("gy")

    def device(dx, dy):
        return (lax.rem(gx + nx + dx, nx), lax.rem(gy + ny + dy, ny))

    def exists(dx, dy):
        return (gx + dx >= 0) & (gx + dx < nx) & (gy + dy >= 0) & (gy + dy < ny)

    sides = ((-1, 0), (1, 0), (0, -1), (0, 1))
    barrier = pltpu.get_barrier_semaphore()
    for side in sides:

        @pl.when(exists(*side))
        def _(side=side):
            pl.semaphore_signal(
                barrier, inc=1, device_id=device(*side), device_id_type=MESH
            )

    loads = [
        pltpu.make_async_copy(source, target, load_sem.at[i])
        for i, (source, target) in enumerate(
            [
                (strength_hbm, strength), (strong_hbm, strong), (colour_hbm, colour), (near_hbm, near),
                (initial_hbm, initial), (blocks_hbm, blocks), (forcing_hbm, forcing), (faces_hbm, faces),
            ]
        )
    ]
    for load in loads:
        load.start()

    left = left_lanes((N, 128))
    blank = jnp.zeros((N, 128), BF16)

    def y_copy(t, b, h):
        slot = 2 * (1 - b) + h
        return pltpu.make_async_remote_copy(
            src_ref=state.at[t, b, h],
            dst_ref=halo.at[t, slot],
            send_sem=send_sem.at[t, slot],
            recv_sem=recv_sem.at[t, slot],
            device_id=device(0, 2 * b - 1),
            device_id_type=MESH,
        )

    def x_copy(t, side):
        return pltpu.make_async_remote_copy(
            src_ref=cross.at[t, side],
            dst_ref=halo.at[t, 5 - side],
            send_sem=send_sem.at[t, 5 - side],
            recv_sem=recv_sem.at[t, 5 - side],
            device_id=device(2 * side - 1, 0),
            device_id_type=MESH,
        )

    def y_start(t, b, h):
        @pl.when(exists(0, 2 * b - 1))
        def _():
            y_copy(t, b, h).start()

    def x_start(t):
        cross[t, 0] = jnp.where(left, state[t, 0, 0], swap(state[t, 1, 0]))
        cross[t, 1] = jnp.where(left, swap(state[t, 0, 1]), state[t, 1, 1])
        for side in range(2):

            @pl.when(exists(2 * side - 1, 0))
            def _(side=side):
                x_copy(t, side).start()

    nothing = jnp.zeros((STEPS, 2, N, 128), F32)
    for b in range(2):

        @pl.when(jnp.logical_not(exists(0, 2 * b - 1)))
        def _(b=b):
            halo[:, pl.ds(2 * b, 2)] = nothing

        @pl.when(jnp.logical_not(exists(2 * b - 1, 0)))
        def _(b=b):
            halo[:, 4 + b] = nothing[:, 0]

    for load in loads[:4]:
        load.wait()
    lane = lax.broadcasted_iota(jnp.int32, (8, 128), 1)
    column = lax.broadcasted_iota(jnp.int32, (8, 128), 0)
    loose[...] = jnp.zeros_like(loose)
    for a in range(4):
        for b in range(2):
            weight = jnp.where(
                near[a, b] == 48, 0.0, strength[a, b] * strong[a, b].astype(F32)
            )
            for s in range(2):
                loose[s, pl.ds(2 * a + b, 1), pl.ds(0, 6)] = weight[s : s + 1]
            loose[2, pl.ds(2 * a + b, 1), pl.ds(0, 4)] = colour[b, 0:1].astype(F32)
    painted = pick(loose[2], column // 2)
    for c in range(2):
        weight = jnp.where(painted == c, loose[0], loose[1])
        for i, face in enumerate((0, 4, 2)):
            rows[pl.ds(8 * c, 8), pl.ds(128 * i, 128)] = pick(weight, lane // N + face)
    rows[pl.ds(0, 8), pl.ds(384, 128)] = painted

    loads[4].wait()
    for b in range(2):
        for h in range(2):
            unpack_pair(initial, rows, state.at[0], b, h, 1.0)
    for load in loads[5:]:
        load.wait()
    for i, face in enumerate((0, 4, 2)):
        both = jnp.concatenate([faces[face], faces[face + 1]], axis=1)
        spread[:, pl.ds(128 * i, 128)] = triple(jnp.concatenate([both, both], axis=0))

    def greet():
        pl.semaphore_wait(barrier, sum(jnp.where(exists(*side), 1, 0) for side in sides))
        for b in range(2):
            for h in range(2):
                y_start(0, b, h)
        x_start(0)

    def setup(c):
        paint = c.astype(F32)
        for b in range(2):
            for h in range(2):
                unpack_pair(blocks, rows, grid, b, h, paint)
                unpack_pair(forcing, rows, known.at[c], b, h, paint)

        def visit(k):
            @pl.when((c == 0) & (k == GREET))
            def _():
                greet()

        invert(grid, visit)
        for b in range(2):
            for h in range(2):
                inverse = grid[b, h]
                stacked = jnp.concatenate(
                    [jnp.where(left, inverse, 0.0), jnp.where(left, 0.0, inverse)], axis=0
                )
                high, low = parts(stacked)
                operand = jnp.concatenate([high, low, high], axis=1)
                target = known[c, b, h]
                lines = triple(jnp.concatenate([target, target], axis=0))
                known[c, b, h] = product(operand, lines)
                mixed = jnp.dot(operand, spread[...], preferred_element_type=F32)
                for low_x in range(2):
                    at = pl.ds(N * low_x, N)
                    weight = rows[pl.ds(8 * c + (2 * h + low_x) * 2 + b, 1), pl.ds(0, 384)]
                    scaled = mixed[N * low_x : N * low_x + N] * weight
                    beside_x, beside_z = scaled[:, :128], scaled[:, 128:256]
                    beside_y = scaled[:, 256:]
                    if b == 0:
                        beside_y = swap(beside_y)
                    inner = jnp.where(left, beside_z + swap(beside_z), swap(beside_y))
                    for i, value in enumerate((inner, beside_x)):
                        high, low = parts(value)
                        for j, part in enumerate((high, low, high)):
                            couple[c, b, h, at, pl.ds(384 * i + 128 * j, 128)] = part
                    high = beside_y.astype(BF16).astype(F32)
                    low = beside_y - high
                    couple[c, b, h, at, pl.ds(768, 128)] = jnp.where(
                        left, swap(high), low
                    ).astype(BF16)
                    couple[c, b, h, at, pl.ds(896, 128)] = jnp.where(
                        left, swap(high), 0.0
                    ).astype(BF16)

    later = lax.rem(gy + 1, 2)

    def sweep(t, carry):
        c = lax.rem(t, 2)

        @pl.when(t < 2)
        def _():
            setup(c)

        for b in range(2):
            for h in range(2):
                beside = jnp.concatenate([state[t, b, h], state[t, 1 - b, h]], axis=0)
                partial[b, h] = known[c, b, h] - product(
                    couple[c, b, h, :, pl.ds(0, 384)], triple(beside)
                )
        for side in range(2):

            @pl.when(exists(2 * side - 1, 0))
            def _(side=side):
                x_copy(t, 1 - side).wait_recv()

        for b in range(2):
            one, two = state[t, b, 0], state[t, b, 1]
            before, after = halo[t, 4], halo[t, 5]
            if b == 0:
                after = swap(after)
            else:
                before = swap(before)
            slides = [
                jnp.where(left, before, swap(one)),
                swap(jnp.where(left, two, one)),
                jnp.where(left, swap(two), after),
            ]
            for h in range(2):
                beside = jnp.concatenate([slides[h], slides[h + 1]], axis=0)
                partial[b, h] = partial[b, h] - product(
                    couple[c, b, h, :, pl.ds(384, 384)], triple(beside)
                )
        for i in range(2):
            b = lax.rem(later + i, 2)

            for h in range(2):

                @pl.when(exists(0, 2 * b - 1))
                def _(b=b, h=h):
                    y_copy(t, 1 - b, h).wait_recv()

                lines = jnp.concatenate([triple(halo[t, 2 * b + h]), blank], axis=0)
                state[t + 1, b, h] = partial[b, h] - product(
                    couple[c, b, h, :, pl.ds(768, 256)], lines
                )

                @pl.when(t < STEPS - 1)
                def _(b=b, h=h):
                    y_start(t + 1, b, h)

        @pl.when(t < STEPS - 1)
        def _():
            x_start(t + 1)

        return carry

    lax.fori_loop(0, STEPS, sweep, 0)

    small = left_lanes((32, 128))
    for b in range(2):
        for h in range(2):
            values = []
            for c in range(2):
                even = state[STEPS - 1 + c, b, h, pl.ds(0, 32, stride=2), :]
                odd = state[STEPS - 1 + c, b, h, pl.ds(1, 32, stride=2), :]
                values.append(
                    (jnp.where(small, even, swap(odd)), jnp.where(small, swap(even), odd))
                )
            for low_x in range(2):
                a = 2 * h + low_x
                first = rows[pl.ds(a * 2 + b, 1), pl.ds(384, 128)]
                first = jnp.broadcast_to(first, (32, 128)) == 0.0
                zero, one = values[0][low_x], values[1][low_x]
                out[a, b, pl.ds(0, 32, stride=2), :] = jnp.where(first, zero, one)
                out[a, b, pl.ds(1, 32, stride=2), :] = jnp.where(first, one, zero)

    def drain(t, carry):
        for b in range(2):

            @pl.when(exists(0, 2 * b - 1))
            def _(b=b):
                for h in range(2):
                    y_copy(t, b, h).wait_send()

            @pl.when(exists(2 * b - 1, 0))
            def _(b=b):
                x_copy(t, b).wait_send()

        return carry

    lax.fori_loop(0, STEPS, drain, 0)


def body(forcing, initial, blocks, face_blocks, strength, strong, colour, neighbours):
    sx, sy, sz, width = forcing.shape
    chunks = width // 128

    def packed(array):
        split = array.reshape(sx, sy, sz, chunks, 128).transpose(0, 1, 3, 2, 4)
        return split.reshape(sx, sy, chunks * sz, 128)

    far = pl.BlockSpec(memory_space=pltpu.HBM)
    large = (sx, sy, chunks * sz, 128)
    result = pl.pallas_call(
        kernel,
        out_shape=jax.ShapeDtypeStruct(large, F32),
        in_specs=[far] * 8,
        out_specs=pl.BlockSpec(memory_space=pltpu.VMEM),
        scratch_shapes=[
            pltpu.VMEM(large, F32),
            pltpu.VMEM(large, F32),
            pltpu.VMEM(large, F32),
            pltpu.VMEM((6, N, N), F32),
            pltpu.VMEM((sx, sy, sz, 6), F32),
            pltpu.VMEM((sx, sy, sz, 6), jnp.int32),
            pltpu.VMEM((sy, sz, sx), jnp.int32),
            pltpu.VMEM((sx, sy, sz, 6), jnp.int32),
            pltpu.SemaphoreType.DMA((8,)),
            pltpu.VMEM((16, 512), F32),
            pltpu.VMEM((3, 8, 128), F32),
            pltpu.VMEM((STEPS + 1, 2, 2, N, 128), F32),
            pltpu.VMEM((STEPS, 2, N, 128), F32),
            pltpu.VMEM((STEPS, 6, N, 128), F32),
            pltpu.VMEM((2, 2, N, 128), F32),
            pltpu.VMEM((2, 2, 2, 2 * N, 1024), BF16),
            pltpu.VMEM((2, 2, 2, N, 128), F32),
            pltpu.VMEM((2, 2, N, 128), F32),
            pltpu.VMEM((6 * N, 6 * N), BF16),
            pltpu.SemaphoreType.DMA((STEPS, 6)),
            pltpu.SemaphoreType.DMA((STEPS, 6)),
        ],
        compiler_params=pltpu.CompilerParams(
            collective_id=0, has_side_effects=True, vmem_limit_bytes=65280 * 2**10
        ),
    )(
        packed(forcing),
        packed(initial),
        packed(blocks),
        face_blocks,
        strength.transpose(1, 2, 3, 0),
        strong.transpose(1, 2, 3, 0),
        colour.transpose(1, 2, 0),
        neighbours.transpose(1, 2, 3, 0),
    )
    result = result.reshape(sx, sy, chunks, sz, 128).transpose(0, 1, 3, 2, 4)
    return result.reshape(sx, sy, sz, width)


def solution(mesh):
    in_specs = (
        P("gx", "gy", None, None),
        P("gx", "gy", None, None),
        P("gx", "gy", None, None),
        P(),
        P(None, "gx", "gy", None),
        P(None, "gx", "gy", None),
        P("gx", "gy", None),
        P(None, "gx", "gy", None),
    )
    out_specs = P("gx", "gy", None, None)
    return jax.shard_map(body, mesh=mesh, in_specs=in_specs, out_specs=out_specs, check_vma=False)
```

```python
import jax
import jax.numpy as jnp
from jax import lax
from jax.experimental import pallas as pl
from jax.experimental.pallas import tpu as pltpu
from jax.sharding import PartitionSpec as P

MESH = pl.DeviceIdType.MESH
N = 64
STEPS = 8
GREET = 2
F32 = jnp.float32
BF16 = jnp.bfloat16


def left_lanes(shape):
    return lax.broadcasted_iota(jnp.int32, shape, len(shape) - 1) < N


def swap(tile):
    return pltpu.roll(tile, N, tile.ndim - 1)


def pick(tile, index):
    return jnp.take_along_axis(tile, index, axis=1)


def spread_row(tile, j):
    return jnp.broadcast_to(tile[j : j + 1, :], tile.shape)


def parts(value):
    high = value.astype(BF16)
    return high, (value - high.astype(F32)).astype(BF16)


def triple(value):
    high, low = parts(value)
    return jnp.concatenate([high, high, low], axis=0)


def product(operand, lines):
    total = jnp.dot(operand, lines, preferred_element_type=F32)
    return jnp.where(left_lanes((N, 128)), total[:N], total[N:])


def unpack_pair(source, rows, target, b, h, paint):
    halves = []
    for low in range(2):
        a = 2 * h + low
        first = jnp.broadcast_to(rows[pl.ds(a * 2 + b, 1), pl.ds(384, 128)], (32, 128))
        zero = source[a, b, pl.ds(0, 32, stride=2), :]
        one = source[a, b, pl.ds(1, 32, stride=2), :]
        halves.append(jnp.where(first == paint, zero, one))
    left = left_lanes((32, 128))
    target[b, h, pl.ds(0, 32, stride=2), :] = jnp.where(left, halves[0], swap(halves[1]))
    target[b, h, pl.ds(1, 32, stride=2), :] = jnp.where(left, swap(halves[0]), halves[1])


def invert(grid, visit):
    places = [(b, h) for b in range(2) for h in range(2)]
    lane = lax.broadcasted_iota(jnp.int32, (8, 128), 1)
    row = lax.broadcasted_iota(jnp.int32, (8, 128), 0)
    within = lax.rem(lane, N)
    start = lane - within
    segment = within // 16
    left = lane < N
    wide = lax.broadcasted_iota(jnp.int32, (N, 128), 1)
    slot = wide // 16
    first = (slot == 0) | (slot == 1) | (slot == 3)
    second = (slot == 2) | (slot == 4)
    third = slot == 5
    base = jnp.where(lax.rem(wide, 16) < 8, 0, N) + lax.rem(wide, 8)

    def block(k, carry):
        visit(k)
        here = pl.ds(pl.multiple_of(8 * k, 8), 8)
        panels = [grid[b, h, here, :] for b, h in places]
        columns = []
        for j in range(8):
            index = start + 8 * k + j
            column = pick(panels[3], index)
            for e in range(3):
                column = jnp.where(segment == e, pick(panels[e], index), column)
            columns.append(column)
        operands = []
        for b, h in places:
            value = pick(grid[b, h], base + 8 * k)
            part1 = value.astype(BF16).astype(F32)
            part2 = (value - part1).astype(BF16).astype(F32)
            part3 = value - part1 - part2
            operand = jnp.where(third, part3, 0.0)
            operand = jnp.where(first, part1, jnp.where(second, part2, operand))
            operands.append(operand.astype(BF16))
        for pivot in range(8):
            lines = [spread_row(column, pivot) for column in columns]
            scale = 1.0 / lines[pivot]
            factor = columns[pivot]
            for j in range(8):
                scaled = scale if j == pivot else lines[j] * scale
                rest = -(factor * scaled) if j == pivot else columns[j] - factor * scaled
                columns[j] = jnp.where(row == pivot, scaled, rest)
        inside = (within >= 8 * k) & (within < 8 * k + 8)
        inside_wide = (lax.rem(wide, N) >= 8 * k) & (lax.rem(wide, N) < 8 * k + 8)
        for e, (b, h) in enumerate(places):
            panel = jnp.zeros((8, 128), F32)
            for j in range(8):
                unit = jnp.where(within == 8 * k + j, 1.0, 0.0)
                value = jnp.where(inside, unit, spread_row(panels[e], j))
                panel = panel + pick(columns[j], start + 16 * e) * value
            both = jnp.concatenate(
                [jnp.where(left, panel, 0.0), jnp.where(left, 0.0, panel)], axis=0
            )
            part1 = both.astype(BF16)
            rest = both - part1.astype(F32)
            part2, part3 = parts(rest)
            nothing = jnp.zeros((32, 128), BF16)
            lines = jnp.concatenate(
                [part1, part2, part1, part3, part2, part1, nothing], axis=0
            )
            update = jnp.dot(operands[e], lines, preferred_element_type=F32)
            grid[b, h] = jnp.where(inside_wide, 0.0, grid[b, h]) - update
            grid[b, h, here, :] = panel
        return carry

    lax.fori_loop(0, 8, block, 0)


def kernel(
    forcing_hbm, initial_hbm, blocks_hbm, faces_hbm, strength_hbm, strong_hbm, colour_hbm, near_hbm,
    out,
    forcing, initial, blocks, faces, strength, strong, colour, near, load_sem,
    rows, loose, state, cross, halo, grid, couple, known, partial, spread, send_sem, recv_sem,
):
    gx, gy = lax.axis_index("gx"), lax.axis_index("gy")
    nx, ny = lax.axis_size("gx"), lax.axis_size("gy")

    def device(dx, dy):
        return (lax.rem(gx + nx + dx, nx), lax.rem(gy + ny + dy, ny))

    def exists(dx, dy):
        return (gx + dx >= 0) & (gx + dx < nx) & (gy + dy >= 0) & (gy + dy < ny)

    sides = ((-1, 0), (1, 0), (0, -1), (0, 1))
    barrier = pltpu.get_barrier_semaphore()
    for side in sides:

        @pl.when(exists(*side))
        def _(side=side):
            pl.semaphore_signal(
                barrier, inc=1, device_id=device(*side), device_id_type=MESH
            )

    loads = [
        pltpu.make_async_copy(source, target, load_sem.at[i])
        for i, (source, target) in enumerate(
            [
                (strength_hbm, strength), (strong_hbm, strong), (colour_hbm, colour), (near_hbm, near),
                (initial_hbm, initial), (blocks_hbm, blocks), (forcing_hbm, forcing), (faces_hbm, faces),
            ]
        )
    ]
    for load in loads:
        load.start()

    left = left_lanes((N, 128))
    blank = jnp.zeros((N, 128), BF16)

    def y_copy(t, b, h):
        slot = 2 * (1 - b) + h
        return pltpu.make_async_remote_copy(
            src_ref=state.at[t, b, h],
            dst_ref=halo.at[t, slot],
            send_sem=send_sem.at[t, slot],
            recv_sem=recv_sem.at[t, slot],
            device_id=device(0, 2 * b - 1),
            device_id_type=MESH,
        )

    def x_copy(t, side):
        return pltpu.make_async_remote_copy(
            src_ref=cross.at[t, side],
            dst_ref=halo.at[t, 5 - side],
            send_sem=send_sem.at[t, 5 - side],
            recv_sem=recv_sem.at[t, 5 - side],
            device_id=device(2 * side - 1, 0),
            device_id_type=MESH,
        )

    def y_start(t, b, h):
        @pl.when(exists(0, 2 * b - 1))
        def _():
            y_copy(t, b, h).start()

    def x_start(t):
        cross[t, 0] = jnp.where(left, state[t, 0, 0], swap(state[t, 1, 0]))
        cross[t, 1] = jnp.where(left, swap(state[t, 0, 1]), state[t, 1, 1])
        for side in range(2):

            @pl.when(exists(2 * side - 1, 0))
            def _(side=side):
                x_copy(t, side).start()

    nothing = jnp.zeros((STEPS, 2, N, 128), F32)
    for b in range(2):

        @pl.when(jnp.logical_not(exists(0, 2 * b - 1)))
        def _(b=b):
            halo[:, pl.ds(2 * b, 2)] = nothing

        @pl.when(jnp.logical_not(exists(2 * b - 1, 0)))
        def _(b=b):
            halo[:, 4 + b] = nothing[:, 0]

    for load in loads[:4]:
        load.wait()
    lane = lax.broadcasted_iota(jnp.int32, (8, 128), 1)
    column = lax.broadcasted_iota(jnp.int32, (8, 128), 0)
    loose[...] = jnp.zeros_like(loose)
    for a in range(4):
        for b in range(2):
            weight = jnp.where(
                near[a, b] == 48, 0.0, strength[a, b] * strong[a, b].astype(F32)
            )
            for s in range(2):
                loose[s, pl.ds(2 * a + b, 1), pl.ds(0, 6)] = weight[s : s + 1]
            loose[2, pl.ds(2 * a + b, 1), pl.ds(0, 4)] = colour[b, 0:1].astype(F32)
    painted = pick(loose[2], column // 2)
    for c in range(2):
        weight = jnp.where(painted == c, loose[0], loose[1])
        for i, face in enumerate((0, 4, 2)):
            rows[pl.ds(8 * c, 8), pl.ds(128 * i, 128)] = pick(weight, lane // N + face)
    rows[pl.ds(0, 8), pl.ds(384, 128)] = painted

    loads[4].wait()
    for b in range(2):
        for h in range(2):
            unpack_pair(initial, rows, state.at[0], b, h, 1.0)
    for load in loads[5:]:
        load.wait()
    for i, face in enumerate((0, 4, 2)):
        both = jnp.concatenate([faces[face], faces[face + 1]], axis=1)
        spread[:, pl.ds(128 * i, 128)] = triple(jnp.concatenate([both, both], axis=0))

    def greet():
        pl.semaphore_wait(barrier, sum(jnp.where(exists(*side), 1, 0) for side in sides))
        for b in range(2):
            for h in range(2):
                y_start(0, b, h)
        x_start(0)

    def setup(c):
        paint = c.astype(F32)
        for b in range(2):
            for h in range(2):
                unpack_pair(blocks, rows, grid, b, h, paint)
                unpack_pair(forcing, rows, known.at[c], b, h, paint)

        def visit(k):
            @pl.when((c == 0) & (k == GREET))
            def _():
                greet()

        invert(grid, visit)
        for b in range(2):
            for h in range(2):
                inverse = grid[b, h]
                stacked = jnp.concatenate(
                    [jnp.where(left, inverse, 0.0), jnp.where(left, 0.0, inverse)], axis=0
                )
                high, low = parts(stacked)
                operand = jnp.concatenate([high, low, high], axis=1)
                target = known[c, b, h]
                lines = triple(jnp.concatenate([target, target], axis=0))
                known[c, b, h] = product(operand, lines)
                mixed = jnp.dot(operand, spread[...], preferred_element_type=F32)
                for low_x in range(2):
                    at = pl.ds(N * low_x, N)
                    weight = rows[pl.ds(8 * c + (2 * h + low_x) * 2 + b, 1), pl.ds(0, 384)]
                    scaled = mixed[N * low_x : N * low_x + N] * weight
                    beside_x, beside_z = scaled[:, :128], scaled[:, 128:256]
                    beside_y = scaled[:, 256:]
                    if b == 0:
                        beside_y = swap(beside_y)
                    inner = jnp.where(left, beside_z + swap(beside_z), swap(beside_y))
                    for i, value in enumerate((inner, beside_x)):
                        high, low = parts(value)
                        for j, part in enumerate((high, low, high)):
                            couple[c, b, h, at, pl.ds(384 * i + 128 * j, 128)] = part
                    high = beside_y.astype(BF16).astype(F32)
                    low = beside_y - high
                    couple[c, b, h, at, pl.ds(768, 128)] = jnp.where(
                        left, swap(high), low
                    ).astype(BF16)
                    couple[c, b, h, at, pl.ds(896, 128)] = jnp.where(
                        left, swap(high), 0.0
                    ).astype(BF16)

    later = lax.rem(gy + 1, 2)

    def sweep(t, carry):
        c = lax.rem(t, 2)

        @pl.when(t < 2)
        def _():
            setup(c)

        for b in range(2):
            for h in range(2):
                beside = jnp.concatenate([state[t, b, h], state[t, 1 - b, h]], axis=0)
                partial[b, h] = known[c, b, h] - product(
                    couple[c, b, h, :, pl.ds(0, 384)], triple(beside)
                )
        for side in range(2):

            @pl.when(exists(2 * side - 1, 0))
            def _(side=side):
                x_copy(t, 1 - side).wait_recv()

        for b in range(2):
            one, two = state[t, b, 0], state[t, b, 1]
            before, after = halo[t, 4], halo[t, 5]
            if b == 0:
                after = swap(after)
            else:
                before = swap(before)
            slides = [
                jnp.where(left, before, swap(one)),
                swap(jnp.where(left, two, one)),
                jnp.where(left, swap(two), after),
            ]
            for h in range(2):
                beside = jnp.concatenate([slides[h], slides[h + 1]], axis=0)
                partial[b, h] = partial[b, h] - product(
                    couple[c, b, h, :, pl.ds(384, 384)], triple(beside)
                )
        for i in range(2):
            b = lax.rem(later + i, 2)

            for h in range(2):

                @pl.when(exists(0, 2 * b - 1))
                def _(b=b, h=h):
                    y_copy(t, 1 - b, h).wait_recv()

                lines = jnp.concatenate([triple(halo[t, 2 * b + h]), blank], axis=0)
                state[t + 1, b, h] = partial[b, h] - product(
                    couple[c, b, h, :, pl.ds(768, 256)], lines
                )

                @pl.when(t < STEPS - 1)
                def _(b=b, h=h):
                    y_start(t + 1, b, h)

        @pl.when(t < STEPS - 1)
        def _():
            x_start(t + 1)

        return carry

    lax.fori_loop(0, STEPS, sweep, 0)

    small = left_lanes((32, 128))
    for b in range(2):
        for h in range(2):
            values = []
            for c in range(2):
                even = state[STEPS - 1 + c, b, h, pl.ds(0, 32, stride=2), :]
                odd = state[STEPS - 1 + c, b, h, pl.ds(1, 32, stride=2), :]
                values.append(
                    (jnp.where(small, even, swap(odd)), jnp.where(small, swap(even), odd))
                )
            for low_x in range(2):
                a = 2 * h + low_x
                first = rows[pl.ds(a * 2 + b, 1), pl.ds(384, 128)]
                first = jnp.broadcast_to(first, (32, 128)) == 0.0
                zero, one = values[0][low_x], values[1][low_x]
                out[a, b, pl.ds(0, 32, stride=2), :] = jnp.where(first, zero, one)
                out[a, b, pl.ds(1, 32, stride=2), :] = jnp.where(first, one, zero)

    def drain(t, carry):
        for b in range(2):

            @pl.when(exists(0, 2 * b - 1))
            def _(b=b):
                for h in range(2):
                    y_copy(t, b, h).wait_send()

            @pl.when(exists(2 * b - 1, 0))
            def _(b=b):
                x_copy(t, b).wait_send()

        return carry

    lax.fori_loop(0, STEPS, drain, 0)


def body(forcing, initial, blocks, face_blocks, strength, strong, colour, neighbours):
    sx, sy, sz, width = forcing.shape
    chunks = width // 128

    def packed(array):
        split = array.reshape(sx, sy, sz, chunks, 128).transpose(0, 1, 3, 2, 4)
        return split.reshape(sx, sy, chunks * sz, 128)

    far = pl.BlockSpec(memory_space=pltpu.HBM)
    large = (sx, sy, chunks * sz, 128)
    result = pl.pallas_call(
        kernel,
        out_shape=jax.ShapeDtypeStruct(large, F32),
        in_specs=[far] * 8,
        out_specs=pl.BlockSpec(memory_space=pltpu.VMEM),
        scratch_shapes=[
            pltpu.VMEM(large, F32),
            pltpu.VMEM(large, F32),
            pltpu.VMEM(large, F32),
            pltpu.VMEM((6, N, N), F32),
            pltpu.VMEM((sx, sy, sz, 6), F32),
            pltpu.VMEM((sx, sy, sz, 6), jnp.int32),
            pltpu.VMEM((sy, sz, sx), jnp.int32),
            pltpu.VMEM((sx, sy, sz, 6), jnp.int32),
            pltpu.SemaphoreType.DMA((8,)),
            pltpu.VMEM((16, 512), F32),
            pltpu.VMEM((3, 8, 128), F32),
            pltpu.VMEM((STEPS + 1, 2, 2, N, 128), F32),
            pltpu.VMEM((STEPS, 2, N, 128), F32),
            pltpu.VMEM((STEPS, 6, N, 128), F32),
            pltpu.VMEM((2, 2, N, 128), F32),
            pltpu.VMEM((2, 2, 2, 2 * N, 1024), BF16),
            pltpu.VMEM((2, 2, 2, N, 128), F32),
            pltpu.VMEM((2, 2, N, 128), F32),
            pltpu.VMEM((6 * N, 6 * N), BF16),
            pltpu.SemaphoreType.DMA((STEPS, 6)),
            pltpu.SemaphoreType.DMA((STEPS, 6)),
        ],
        compiler_params=pltpu.CompilerParams(
            collective_id=0, has_side_effects=True, vmem_limit_bytes=40000 * 2**10
        ),
    )(
        *(
            pltpu.with_memory_space_constraint(array, pltpu.HBM)
            for array in (
                packed(forcing),
                packed(initial),
                packed(blocks),
                face_blocks,
                strength.transpose(1, 2, 3, 0),
                strong.transpose(1, 2, 3, 0),
                colour.transpose(1, 2, 0),
                neighbours.transpose(1, 2, 3, 0),
            )
        )
    )
    result = result.reshape(sx, sy, chunks, sz, 128).transpose(0, 1, 3, 2, 4)
    return result.reshape(sx, sy, sz, width)


def solution(mesh):
    in_specs = (
        P("gx", "gy", None, None),
        P("gx", "gy", None, None),
        P("gx", "gy", None, None),
        P(),
        P(None, "gx", "gy", None),
        P(None, "gx", "gy", None),
        P("gx", "gy", None),
        P(None, "gx", "gy", None),
    )
    out_specs = P("gx", "gy", None, None)
    return jax.shard_map(body, mesh=mesh, in_specs=in_specs, out_specs=out_specs, check_vma=False)
```

```python
import jax
import jax.numpy as jnp
from jax import lax
from jax.experimental import pallas as pl
from jax.experimental.pallas import tpu as pltpu
from jax.sharding import PartitionSpec as P

MESH = pl.DeviceIdType.MESH
N = 64
STEPS = 8
GREET = 2
F32 = jnp.float32
BF16 = jnp.bfloat16


def left_lanes(shape):
    return lax.broadcasted_iota(jnp.int32, shape, len(shape) - 1) < N


def swap(tile):
    return pltpu.roll(tile, N, tile.ndim - 1)


def pick(tile, index):
    return jnp.take_along_axis(tile, index, axis=1)


def spread_row(tile, j):
    return jnp.broadcast_to(tile[j : j + 1, :], tile.shape)


def parts(value):
    high = value.astype(BF16)
    return high, (value - high.astype(F32)).astype(BF16)


def triple(value):
    high, low = parts(value)
    return jnp.concatenate([high, high, low], axis=0)


def product(operand, lines):
    total = jnp.dot(operand, lines, preferred_element_type=F32)
    return jnp.where(left_lanes((N, 128)), total[:N], total[N:])


def unpack_pair(source, rows, target, b, h, paint):
    halves = []
    for low in range(2):
        a = 2 * h + low
        first = jnp.broadcast_to(rows[pl.ds(a * 2 + b, 1), pl.ds(384, 128)], (32, 128))
        zero = source[a, b, pl.ds(0, 32, stride=2), :]
        one = source[a, b, pl.ds(1, 32, stride=2), :]
        halves.append(jnp.where(first == paint, zero, one))
    left = left_lanes((32, 128))
    target[b, h, pl.ds(0, 32, stride=2), :] = jnp.where(left, halves[0], swap(halves[1]))
    target[b, h, pl.ds(1, 32, stride=2), :] = jnp.where(left, swap(halves[0]), halves[1])


def invert(grid, visit):
    places = [(b, h) for b in range(2) for h in range(2)]
    lane = lax.broadcasted_iota(jnp.int32, (8, 128), 1)
    row = lax.broadcasted_iota(jnp.int32, (8, 128), 0)
    within = lax.rem(lane, N)
    start = lane - within
    segment = within // 16
    left = lane < N
    wide = lax.broadcasted_iota(jnp.int32, (N, 128), 1)
    slot = wide // 16
    first = (slot == 0) | (slot == 1) | (slot == 3)
    second = (slot == 2) | (slot == 4)
    third = slot == 5
    base = jnp.where(lax.rem(wide, 16) < 8, 0, N) + lax.rem(wide, 8)

    def block(k, carry):
        visit(k)
        here = pl.ds(pl.multiple_of(8 * k, 8), 8)
        panels = [grid[b, h, here, :] for b, h in places]
        columns = []
        for j in range(8):
            index = start + 8 * k + j
            column = pick(panels[3], index)
            for e in range(3):
                column = jnp.where(segment == e, pick(panels[e], index), column)
            columns.append(column)
        operands = []
        for b, h in places:
            value = pick(grid[b, h], base + 8 * k)
            part1 = value.astype(BF16).astype(F32)
            part2 = (value - part1).astype(BF16).astype(F32)
            part3 = value - part1 - part2
            operand = jnp.where(third, part3, 0.0)
            operand = jnp.where(first, part1, jnp.where(second, part2, operand))
            operands.append(operand.astype(BF16))
        for pivot in range(8):
            lines = [spread_row(column, pivot) for column in columns]
            scale = 1.0 / lines[pivot]
            factor = columns[pivot]
            for j in range(8):
                scaled = scale if j == pivot else lines[j] * scale
                rest = -(factor * scaled) if j == pivot else columns[j] - factor * scaled
                columns[j] = jnp.where(row == pivot, scaled, rest)
        inside = (within >= 8 * k) & (within < 8 * k + 8)
        inside_wide = (lax.rem(wide, N) >= 8 * k) & (lax.rem(wide, N) < 8 * k + 8)
        for e, (b, h) in enumerate(places):
            panel = jnp.zeros((8, 128), F32)
            for j in range(8):
                unit = jnp.where(within == 8 * k + j, 1.0, 0.0)
                value = jnp.where(inside, unit, spread_row(panels[e], j))
                panel = panel + pick(columns[j], start + 16 * e) * value
            both = jnp.concatenate(
                [jnp.where(left, panel, 0.0), jnp.where(left, 0.0, panel)], axis=0
            )
            part1 = both.astype(BF16)
            rest = both - part1.astype(F32)
            part2, part3 = parts(rest)
            nothing = jnp.zeros((32, 128), BF16)
            lines = jnp.concatenate(
                [part1, part2, part1, part3, part2, part1, nothing], axis=0
            )
            update = jnp.dot(operands[e], lines, preferred_element_type=F32)
            grid[b, h] = jnp.where(inside_wide, 0.0, grid[b, h]) - update
            grid[b, h, here, :] = panel
        return carry

    lax.fori_loop(0, 8, block, 0)


def kernel(
    forcing_hbm, initial_hbm, blocks_hbm, faces_hbm, strength_hbm, strong_hbm, colour_hbm, near_hbm,
    out,
    forcing, initial, blocks, faces, strength, strong, colour, near, load_sem,
    rows, loose, state, cross, halo, grid, couple, known, partial, spread, send_sem, recv_sem,
):
    gx, gy = lax.axis_index("gx"), lax.axis_index("gy")
    nx, ny = lax.axis_size("gx"), lax.axis_size("gy")

    def device(dx, dy):
        return (lax.rem(gx + nx + dx, nx), lax.rem(gy + ny + dy, ny))

    def exists(dx, dy):
        return (gx + dx >= 0) & (gx + dx < nx) & (gy + dy >= 0) & (gy + dy < ny)

    sides = ((-1, 0), (1, 0), (0, -1), (0, 1))
    barrier = pltpu.get_barrier_semaphore()
    for side in sides:

        @pl.when(exists(*side))
        def _(side=side):
            pl.semaphore_signal(
                barrier, inc=1, device_id=device(*side), device_id_type=MESH
            )

    loads = [
        pltpu.make_async_copy(source, target, load_sem.at[i])
        for i, (source, target) in enumerate(
            [
                (strength_hbm, strength), (strong_hbm, strong), (colour_hbm, colour), (near_hbm, near),
                (initial_hbm, initial), (blocks_hbm, blocks), (forcing_hbm, forcing), (faces_hbm, faces),
            ]
        )
    ]
    for load in loads:
        load.start()

    left = left_lanes((N, 128))
    blank = jnp.zeros((N, 128), BF16)

    def y_copy(t, b, h):
        slot = 2 * (1 - b) + h
        return pltpu.make_async_remote_copy(
            src_ref=state.at[t, b, h],
            dst_ref=halo.at[t, slot],
            send_sem=send_sem.at[t, slot],
            recv_sem=recv_sem.at[t, slot],
            device_id=device(0, 2 * b - 1),
            device_id_type=MESH,
        )

    def x_copy(t, side):
        return pltpu.make_async_remote_copy(
            src_ref=cross.at[t, side],
            dst_ref=halo.at[t, 5 - side],
            send_sem=send_sem.at[t, 5 - side],
            recv_sem=recv_sem.at[t, 5 - side],
            device_id=device(2 * side - 1, 0),
            device_id_type=MESH,
        )

    def y_start(t, b, h):
        @pl.when(exists(0, 2 * b - 1))
        def _():
            y_copy(t, b, h).start()

    def x_start(t):
        cross[t, 0] = jnp.where(left, state[t, 0, 0], swap(state[t, 1, 0]))
        cross[t, 1] = jnp.where(left, swap(state[t, 0, 1]), state[t, 1, 1])
        for side in range(2):

            @pl.when(exists(2 * side - 1, 0))
            def _(side=side):
                x_copy(t, side).start()

    nothing = jnp.zeros((STEPS, 2, N, 128), F32)
    for b in range(2):

        @pl.when(jnp.logical_not(exists(0, 2 * b - 1)))
        def _(b=b):
            halo[:, pl.ds(2 * b, 2)] = nothing

        @pl.when(jnp.logical_not(exists(2 * b - 1, 0)))
        def _(b=b):
            halo[:, 4 + b] = nothing[:, 0]

    for load in loads[:4]:
        load.wait()
    lane = lax.broadcasted_iota(jnp.int32, (8, 128), 1)
    column = lax.broadcasted_iota(jnp.int32, (8, 128), 0)
    loose[...] = jnp.zeros_like(loose)
    for a in range(4):
        for b in range(2):
            weight = jnp.where(
                near[a, b] == 48, 0.0, strength[a, b] * strong[a, b].astype(F32)
            )
            for s in range(2):
                loose[s, pl.ds(2 * a + b, 1), pl.ds(0, 6)] = weight[s : s + 1]
            loose[2, pl.ds(2 * a + b, 1), pl.ds(0, 4)] = colour[b, 0:1].astype(F32)
    painted = pick(loose[2], column // 2)
    for c in range(2):
        weight = jnp.where(painted == c, loose[0], loose[1])
        for i, face in enumerate((0, 4, 2)):
            rows[pl.ds(8 * c, 8), pl.ds(128 * i, 128)] = pick(weight, lane // N + face)
    rows[pl.ds(0, 8), pl.ds(384, 128)] = painted

    loads[4].wait()
    for b in range(2):
        for h in range(2):
            unpack_pair(initial, rows, state.at[0], b, h, 1.0)
    for load in loads[5:]:
        load.wait()
    for i, face in enumerate((0, 4, 2)):
        both = jnp.concatenate([faces[face], faces[face + 1]], axis=1)
        spread[:, pl.ds(128 * i, 128)] = triple(jnp.concatenate([both, both], axis=0))

    def greet():
        pl.semaphore_wait(barrier, sum(jnp.where(exists(*side), 1, 0) for side in sides))
        for b in range(2):
            for h in range(2):
                y_start(0, b, h)
        x_start(0)

    def setup(c):
        paint = c.astype(F32)
        for b in range(2):
            for h in range(2):
                unpack_pair(blocks, rows, grid, b, h, paint)
                unpack_pair(forcing, rows, known.at[c], b, h, paint)

        def visit(k):
            @pl.when((c == 0) & (k == GREET))
            def _():
                greet()

        invert(grid, visit)
        for b in range(2):
            for h in range(2):
                inverse = grid[b, h]
                stacked = jnp.concatenate(
                    [jnp.where(left, inverse, 0.0), jnp.where(left, 0.0, inverse)], axis=0
                )
                high, low = parts(stacked)
                operand = jnp.concatenate([high, low, high], axis=1)
                target = known[c, b, h]
                lines = triple(jnp.concatenate([target, target], axis=0))
                known[c, b, h] = product(operand, lines)
                mixed = jnp.dot(operand, spread[...], preferred_element_type=F32)
                for low_x in range(2):
                    at = pl.ds(N * low_x, N)
                    weight = rows[pl.ds(8 * c + (2 * h + low_x) * 2 + b, 1), pl.ds(0, 384)]
                    scaled = mixed[N * low_x : N * low_x + N] * weight
                    beside_x, beside_z = scaled[:, :128], scaled[:, 128:256]
                    beside_y = scaled[:, 256:]
                    if b == 0:
                        beside_y = swap(beside_y)
                    inner = jnp.where(left, beside_z + swap(beside_z), swap(beside_y))
                    for i, value in enumerate((inner, beside_x)):
                        high, low = parts(value)
                        for j, part in enumerate((high, low, high)):
                            couple[c, b, h, at, pl.ds(384 * i + 128 * j, 128)] = part
                    high = beside_y.astype(BF16).astype(F32)
                    low = beside_y - high
                    couple[c, b, h, at, pl.ds(768, 128)] = jnp.where(
                        left, swap(high), low
                    ).astype(BF16)
                    couple[c, b, h, at, pl.ds(896, 128)] = jnp.where(
                        left, swap(high), 0.0
                    ).astype(BF16)

    later = lax.rem(gy + 1, 2)

    def drain(t):
        for b in range(2):

            @pl.when(exists(0, 2 * b - 1))
            def _(b=b):
                for h in range(2):
                    y_copy(t, b, h).wait_send()

            @pl.when(exists(2 * b - 1, 0))
            def _(b=b):
                x_copy(t, b).wait_send()

    def sweep(t, carry):
        c = lax.rem(t, 2)

        @pl.when(t < 2)
        def _():
            setup(c)

        for b in range(2):
            for h in range(2):
                beside = jnp.concatenate([state[t, b, h], state[t, 1 - b, h]], axis=0)
                partial[b, h] = known[c, b, h] - product(
                    couple[c, b, h, :, pl.ds(0, 384)], triple(beside)
                )
        for side in range(2):

            @pl.when(exists(2 * side - 1, 0))
            def _(side=side):
                x_copy(t, 1 - side).wait_recv()

        for b in range(2):
            one, two = state[t, b, 0], state[t, b, 1]
            before, after = halo[t, 4], halo[t, 5]
            if b == 0:
                after = swap(after)
            else:
                before = swap(before)
            slides = [
                jnp.where(left, before, swap(one)),
                swap(jnp.where(left, two, one)),
                jnp.where(left, swap(two), after),
            ]
            for h in range(2):
                beside = jnp.concatenate([slides[h], slides[h + 1]], axis=0)
                partial[b, h] = partial[b, h] - product(
                    couple[c, b, h, :, pl.ds(384, 384)], triple(beside)
                )
        for i in range(2):
            b = lax.rem(later + i, 2)

            for h in range(2):

                @pl.when(exists(0, 2 * b - 1))
                def _(b=b, h=h):
                    y_copy(t, 1 - b, h).wait_recv()

                lines = jnp.concatenate([triple(halo[t, 2 * b + h]), blank], axis=0)
                state[t + 1, b, h] = partial[b, h] - product(
                    couple[c, b, h, :, pl.ds(768, 256)], lines
                )

                @pl.when(t < STEPS - 1)
                def _(b=b, h=h):
                    y_start(t + 1, b, h)

        @pl.when(t < STEPS - 1)
        def _():
            x_start(t + 1)

        drain(t)
        return carry

    lax.fori_loop(0, STEPS, sweep, 0)

    small = left_lanes((32, 128))
    for b in range(2):
        for h in range(2):
            values = []
            for c in range(2):
                even = state[STEPS - 1 + c, b, h, pl.ds(0, 32, stride=2), :]
                odd = state[STEPS - 1 + c, b, h, pl.ds(1, 32, stride=2), :]
                values.append(
                    (jnp.where(small, even, swap(odd)), jnp.where(small, swap(even), odd))
                )
            for low_x in range(2):
                a = 2 * h + low_x
                first = rows[pl.ds(a * 2 + b, 1), pl.ds(384, 128)]
                first = jnp.broadcast_to(first, (32, 128)) == 0.0
                zero, one = values[0][low_x], values[1][low_x]
                out[a, b, pl.ds(0, 32, stride=2), :] = jnp.where(first, zero, one)
                out[a, b, pl.ds(1, 32, stride=2), :] = jnp.where(first, one, zero)


def body(forcing, initial, blocks, face_blocks, strength, strong, colour, neighbours):
    sx, sy, sz, width = forcing.shape
    chunks = width // 128

    def packed(array):
        split = array.reshape(sx, sy, sz, chunks, 128).transpose(0, 1, 3, 2, 4)
        return split.reshape(sx, sy, chunks * sz, 128)

    far = pl.BlockSpec(memory_space=pltpu.HBM)
    large = (sx, sy, chunks * sz, 128)
    result = pl.pallas_call(
        kernel,
        out_shape=jax.ShapeDtypeStruct(large, F32),
        in_specs=[far] * 8,
        out_specs=pl.BlockSpec(memory_space=pltpu.VMEM),
        scratch_shapes=[
            pltpu.VMEM(large, F32),
            pltpu.VMEM(large, F32),
            pltpu.VMEM(large, F32),
            pltpu.VMEM((6, N, N), F32),
            pltpu.VMEM((sx, sy, sz, 6), F32),
            pltpu.VMEM((sx, sy, sz, 6), jnp.int32),
            pltpu.VMEM((sy, sz, sx), jnp.int32),
            pltpu.VMEM((sx, sy, sz, 6), jnp.int32),
            pltpu.SemaphoreType.DMA((8,)),
            pltpu.VMEM((16, 512), F32),
            pltpu.VMEM((3, 8, 128), F32),
            pltpu.VMEM((STEPS + 1, 2, 2, N, 128), F32),
            pltpu.VMEM((STEPS, 2, N, 128), F32),
            pltpu.VMEM((STEPS, 6, N, 128), F32),
            pltpu.VMEM((2, 2, N, 128), F32),
            pltpu.VMEM((2, 2, 2, 2 * N, 1024), BF16),
            pltpu.VMEM((2, 2, 2, N, 128), F32),
            pltpu.VMEM((2, 2, N, 128), F32),
            pltpu.VMEM((6 * N, 6 * N), BF16),
            pltpu.SemaphoreType.DMA((STEPS, 6)),
            pltpu.SemaphoreType.DMA((STEPS, 6)),
        ],
        compiler_params=pltpu.CompilerParams(
            collective_id=0, has_side_effects=True, vmem_limit_bytes=40000 * 2**10
        ),
    )(
        *(
            pltpu.with_memory_space_constraint(array, pltpu.HBM)
            for array in (
                packed(forcing),
                packed(initial),
                packed(blocks),
                face_blocks,
                strength.transpose(1, 2, 3, 0),
                strong.transpose(1, 2, 3, 0),
                colour.transpose(1, 2, 0),
                neighbours.transpose(1, 2, 3, 0),
            )
        )
    )
    result = result.reshape(sx, sy, chunks, sz, 128).transpose(0, 1, 3, 2, 4)
    return result.reshape(sx, sy, sz, width)


def solution(mesh):
    in_specs = (
        P("gx", "gy", None, None),
        P("gx", "gy", None, None),
        P("gx", "gy", None, None),
        P(),
        P(None, "gx", "gy", None),
        P(None, "gx", "gy", None),
        P("gx", "gy", None),
        P(None, "gx", "gy", None),
    )
    out_specs = P("gx", "gy", None, None)
    return jax.shard_map(body, mesh=mesh, in_specs=in_specs, out_specs=out_specs, check_vma=False)
```
